256 devices in a mesh: section: 4 (over x), dp: 64 (over y, z, core).
Axes of the slice: x: 4, y: 4, z: 8, core: 2. Of those that a mesh axis runs over, the one named last changes fastest.
Arguments:
- acts: bfloat16 [4, 8192, 4096], P('section', 'dp'), may hold values from -6 to 6
- grad_rows: bfloat16 [4, 8192, 8192], P('section', 'dp'), may hold values from -6 to 6
- block_experts: int32 [4, 64, 2], P('section'), may hold values from 0 to 7, all different within a row
Outputs:
- weight_grad: bfloat16 [4, 64, 512, 1024], P('section', 'dp')
The draws below stay inside these ranges and needn't reach their ends.
All inputs are finite; a program needn't handle non-finite values.
Results may differ from the reference program's by a relative error of at most 0.001.
Values may be sent and summed in bfloat16 or wider, within the bound.
No kernel may reach another device: no remote copies, remote signals or barrier semaphores. Data moves between devices by JAX's collectives and lax.ppermute only.
A program may use at most 128 MiB of HBM per device.

```python
import math
import jax
import jax.numpy as jnp
from jax import lax

DW = 4096
HW = 8192
E = 8
BLOCK = 128
DGRID = 8
TOKENS = 8192
BLOCKS = 64
HGRID = 8
N_SECTION = 4
N_DP = 64


def steps_of(stream_key, shape, pieces, low, top_value):
    def one(dim, blocks):
        heights = jax.random.uniform(jax.random.fold_in(jax.random.fold_in(stream_key, 6), dim), (blocks,), jnp.float32, low / len(pieces), top_value / len(pieces))
        return jnp.repeat(jnp.exp(heights), shape[dim] // blocks).reshape((-1,) + (1,) * (len(shape) - dim - 1))

    gain = one(*pieces[0])
    for cut in pieces[1:]:
        gain = gain * one(*cut)
    return gain


def choose_distinct(stream_key, rows, amount, top, lift):
    order = jax.random.permutation(jax.random.fold_in(stream_key, 1), amount)
    pull = order
    for power in range(3):
        pull = pull * pull // amount
    pull = pull * lift // amount
    chance = jax.random.randint(jax.random.fold_in(stream_key, 2), (rows, amount), 0, 4096) + pull
    fixed_rows = jax.random.permutation(jax.random.fold_in(stream_key, 3), rows)[jnp.arange(amount) % rows]
    chance = jnp.where(jnp.arange(rows)[:, None] == fixed_rows[None, :], 1 << 14, chance)
    priority = chance * amount + jnp.arange(amount)
    return lax.top_k(priority.astype(jnp.int32), top)[1].astype(jnp.int32)


def noise(own_key, dims, width, most, cuts=(), held_as=jnp.bfloat16):
    result = jax.random.normal(own_key, dims, jnp.float32) * width
    if len(cuts) > 0:
        result = steps_of(own_key, dims, cuts, -0.22, 0.18) * result
    return jnp.clip(result, min=-most, max=most).astype(held_as)


def setup_inputs(seed: int = 0) -> dict:
    seeds = jax.random.split(jax.random.key(seed), 4)
    return {
        "acts": noise(seeds[0], (N_SECTION, TOKENS, DW), 1.0, 6.0, ((0, 4), (1, 64))),
        "grad_rows": noise(seeds[1], (N_SECTION, TOKENS, HW), 1.0, 6.0, ((0, 4), (1, 64))),
        "block_experts": choose_distinct(seeds[2], N_SECTION * BLOCKS, E, 2, 2048).reshape((N_SECTION, BLOCKS, 2)),
    }


def reference(acts, grad_rows, block_experts):
    results = []
    for section in range(N_SECTION):
        acts_now = acts[section]
        grads_now = grad_rows[(section + 1) % N_SECTION]
        touched = jnp.any(block_experts[section] == 0, axis=1)

        def add_block(index, running):

            def with_block(summed):
                start = (index * BLOCK).astype(jnp.int32)
                act_rows = lax.dynamic_slice_in_dim(acts_now, start, BLOCK, 0)
                grad_part = lax.dynamic_slice_in_dim(grads_now, start, BLOCK, 0)
                return summed + lax.dot_general(act_rows, grad_part, (((0,), (0,)), ((), ())), preferred_element_type=jnp.float32)
            return lax.cond(touched[index], with_block, lambda summed: summed, running)
        summed = lax.fori_loop(0, BLOCKS, add_block, jnp.zeros((DW, HW), jnp.float32))
        full = (summed * (2.0 / math.sqrt(TOKENS))).astype(jnp.bfloat16)
        tiles = full.reshape(DGRID, DW // DGRID, HGRID, HW // HGRID).transpose(0, 2, 1, 3)
        results.append(tiles.reshape(N_DP, DW // DGRID, HW // HGRID))
    return jnp.stack(results)
```

```python
import math

import jax
import jax.numpy as jnp
from jax import lax
from jax.experimental import pallas as pl
from jax.experimental.pallas import tpu as pltpu
from jax.sharding import Mesh
from jax.sharding import PartitionSpec as P

DW = 4096
HW = 8192
BLOCK = 128
DGRID = 8
HGRID = 8
BLOCKS = 64
SUB = BLOCK // DGRID
TR = DW // DGRID
TC = HW // HGRID
NY = 4
NX = 4

CAPS = (4, 8, 10, 12, 14, 16, 18, 20, 22, 24, 26, 28, 30, 32, 40, 48, 64)
DP = ("y", "zh", "zl", "core")


def pack_kernel(acts_ref, grads_ref, out_ref):
    for c in range(HGRID):
        out_ref[c, :, :TR] = acts_ref[c * SUB:(c + 1) * SUB, :]
        out_ref[c, :, TR:] = grads_ref[:, c * TC:(c + 1) * TC]


def pack(acts, grads):
    return pl.pallas_call(
        pack_kernel,
        grid=(DGRID,),
        in_specs=[
            pl.BlockSpec((BLOCK, TR), lambda a: (0, a)),
            pl.BlockSpec((SUB, HW), lambda a: (a, 0)),
        ],
        out_specs=pl.BlockSpec((HGRID, SUB, TR + TC), lambda a: (a, 0, 0)),
        out_shape=jax.ShapeDtypeStruct((DGRID * HGRID, SUB, TR + TC), jnp.bfloat16),
    )(acts, grads)


def compact_kernel(cap, aidx, gidx, count, recv, acts_out, grads_out, asem, gsem):
    def acopy(k):
        return pltpu.make_async_copy(recv.at[aidx[k], :, pl.ds(0, TR)], acts_out.at[k], asem.at[k])

    def gcopy(k):
        return pltpu.make_async_copy(recv.at[gidx[k], :, pl.ds(TR, TC)], grads_out.at[k], gsem.at[k])

    def start(k, carry):
        gcopy(k).start()
        acopy(k).start()
        return carry

    def finish(k, carry):
        gcopy(k).wait()
        acopy(k).wait()
        return carry

    lax.fori_loop(0, cap, start, 0)
    lax.fori_loop(0, cap, finish, 0)

    def clear(k, carry):
        acts_out[k] = jnp.zeros((SUB, TR), jnp.bfloat16)
        return carry

    lax.fori_loop(count[0], cap, clear, 0)


def compact(cap, recv, aidx, gidx, count):
    smem = pl.BlockSpec(memory_space=pltpu.SMEM)
    vmem = pl.BlockSpec(memory_space=pltpu.VMEM)
    return pl.pallas_call(
        lambda *refs: compact_kernel(cap, *refs),
        in_specs=[smem, smem, smem, pl.BlockSpec(memory_space=pl.ANY)],
        out_specs=[vmem, vmem],
        out_shape=[
            jax.ShapeDtypeStruct((cap, SUB, TR), jnp.bfloat16),
            jax.ShapeDtypeStruct((cap, SUB, TC), jnp.bfloat16),
        ],
        scratch_shapes=[pltpu.SemaphoreType.DMA((cap,)), pltpu.SemaphoreType.DMA((cap,))],
    )(aidx, gidx, count, recv)


def order_of(touched):
    blocks = jnp.arange(BLOCKS)
    rank = jnp.sum((blocks[None, :] < blocks[:, None]) & touched[None, :], axis=1)
    hit = touched[None, :] & (rank[None, :] == blocks[:, None])
    return jnp.sum(jnp.where(hit, blocks[None, :], 0), axis=1).astype(jnp.int32)


def ring(axis, size, distance):
    return [(i, (i + distance) % size) for i in range(size)]


def branch(cap, recv, aidx, gidx, count):
    y, zh = lax.axis_index("y"), lax.axis_index("zh")
    acts_c, grads_c = compact(cap, recv, aidx, gidx, count)
    near = lax.ppermute(grads_c, "x", ring("x", NX, -1))
    far = lax.ppermute(
        grads_c, ("x", "zh"),
        [(s * 2 + h, ((s - 1) % NX) * 2 + 1 - h) for s in range(NX) for h in range(2)],
    )
    acts_all = lax.all_gather(acts_c, ("zl", "core"))
    half = cap // 2

    def term(piece, behind, flip, low, high):
        a = lax.rem(y + NY - behind, NY) * 2 + (1 - zh if flip else zh)
        acts_part = lax.dynamic_index_in_dim(acts_all, a, 0, keepdims=False)[low:high]
        return lax.dot_general(
            acts_part.reshape(-1, TR), piece.reshape(-1, TC),
            (((0,), (0,)), ((), ())), preferred_element_type=jnp.float32,
        )

    total = None
    for flip, own in ((False, near), (True, far)):
        up = lax.ppermute(own, "y", ring("y", NY, 1))
        down = lax.ppermute(own, "y", ring("y", NY, -1))
        up2 = lax.ppermute(up[:half], "y", ring("y", NY, 1))
        down2 = lax.ppermute(down[half:], "y", ring("y", NY, -1))
        for piece, behind, low, high in (
            (own, 0, 0, cap), (up, 1, 0, cap), (down, 3, 0, cap),
            (up2, 2, 0, half), (down2, 2, half, cap),
        ):
            now = term(piece, behind, flip, low, high)
            total = now if total is None else total + now
    return (total * (2.0 / math.sqrt(BLOCKS * BLOCK))).astype(jnp.bfloat16)


def shards(acts, grad_rows, block_experts):
    packed = pack(acts[0], grad_rows[0])
    behind = [block_experts] + [
        lax.ppermute(block_experts, "x", ring("x", NX, d)) for d in (1, 2, 3)
    ]
    touched = [jnp.any(b[0] == 0, axis=1) for b in behind]
    counts = [jnp.sum(t.astype(jnp.int32)) for t in touched]
    most = jnp.maximum(jnp.maximum(counts[0], counts[1]), jnp.maximum(counts[2], counts[3]))
    which = jnp.sum(most > jnp.array(CAPS[:-1], jnp.int32)).astype(jnp.int32)
    aidx, gidx = order_of(touched[0]), order_of(touched[1])
    recv = lax.all_to_all(packed, DP, split_axis=0, concat_axis=0, tiled=True)
    out = lax.switch(
        which,
        [lambda *o, cap=cap: branch(cap, *o) for cap in CAPS],
        recv, aidx, gidx, counts[0].reshape(1),
    )
    return out[None, None]


def solution(mesh):
    fine = Mesh(mesh.devices.reshape(NX, NY, 2, 4, 2), ("x",) + DP)
    return jax.shard_map(
        shards,
        mesh=fine,
        in_specs=(P("x", DP, None), P("x", DP, None), P("x", None, None)),
        out_specs=P("x", DP, None, None),
        check_vma=False,
    )
```

```python
import math

import jax
import jax.numpy as jnp
from jax import lax
from jax.experimental import pallas as pl
from jax.experimental.pallas import tpu as pltpu
from jax.sharding import Mesh
from jax.sharding import PartitionSpec as P

DW = 4096
HW = 8192
BLOCK = 128
DGRID = 8
HGRID = 8
BLOCKS = 64
SUB = BLOCK // DGRID
TR = DW // DGRID
TC = HW // HGRID
NY = 4
NX = 4

NZ = 8
MTILE = 256

CAPS = (24, 20, 16)
MORE = 32
DP = ("y", "zh", "zl", "core")


def pack_kernel(acts_ref, grads_ref, out_ref):
    for c in range(HGRID):
        out_ref[c, :, :TR] = acts_ref[c * SUB:(c + 1) * SUB, :]
        out_ref[c, :, TR:] = grads_ref[:, c * TC:(c + 1) * TC]


def pack(acts, grads):
    return pl.pallas_call(
        pack_kernel,
        grid=(DGRID,),
        in_specs=[
            pl.BlockSpec((BLOCK, TR), lambda a: (0, a)),
            pl.BlockSpec((SUB, HW), lambda a: (a, 0)),
        ],
        out_specs=pl.BlockSpec((HGRID, SUB, TR + TC), lambda a: (a, 0, 0)),
        out_shape=jax.ShapeDtypeStruct((DGRID * HGRID, SUB, TR + TC), jnp.bfloat16),
    )(acts, grads)


def compact_kernel(cap, aidx, gidx, count, recv, acts_out, grads_out, asem, gsem):
    def acopy(k):
        return pltpu.make_async_copy(recv.at[aidx[k], :, pl.ds(0, TR)], acts_out.at[k], asem.at[k])

    def gcopy(k):
        return pltpu.make_async_copy(recv.at[gidx[k], :, pl.ds(TR, TC)], grads_out.at[k], gsem.at[k])

    def start(k, carry):
        gcopy(k).start()
        acopy(k).start()
        return carry

    def finish(k, carry):
        gcopy(k).wait()
        acopy(k).wait()
        return carry

    lax.fori_loop(0, cap, start, 0)
    lax.fori_loop(0, cap, finish, 0)

    def clear(k, carry):
        acts_out[k] = jnp.zeros((SUB, TR), jnp.bfloat16)
        return carry

    lax.fori_loop(count[0], cap, clear, 0)


def compact(cap, recv, aidx, gidx, count):
    smem = pl.BlockSpec(memory_space=pltpu.SMEM)
    vmem = pl.BlockSpec(memory_space=pltpu.VMEM)
    return pl.pallas_call(
        lambda *refs: compact_kernel(cap, *refs),
        in_specs=[smem, smem, smem, pl.BlockSpec(memory_space=pl.ANY)],
        out_specs=[vmem, vmem],
        out_shape=[
            jax.ShapeDtypeStruct((cap, SUB, TR), jnp.bfloat16),
            jax.ShapeDtypeStruct((cap, SUB, TC), jnp.bfloat16),
        ],
        scratch_shapes=[pltpu.SemaphoreType.DMA((cap,)), pltpu.SemaphoreType.DMA((cap,))],
    )(aidx, gidx, count, recv)


def order_of(touched):
    blocks = jnp.arange(BLOCKS)
    rank = jnp.sum((blocks[None, :] < blocks[:, None]) & touched[None, :], axis=1)
    hit = touched[None, :] & (rank[None, :] == blocks[:, None])
    return jnp.sum(jnp.where(hit, blocks[None, :], 0), axis=1).astype(jnp.int32)


def ring(axis, size, distance):
    return [(i, (i + distance) % size) for i in range(size)]


def product_kernel(n, scale, has_total, *refs):
    where, acts = refs[0], refs[1]
    pieces, rest = refs[2:2 + n], refs[2 + n:]
    out = rest[-1]
    for low in range(0, TR, MTILE):
        total = rest[0][low:low + MTILE, :] if has_total else None
        for i in range(n):
            now = lax.dot_general(
                acts[where[i], :, low:low + MTILE], pieces[i][...],
                (((0,), (0,)), ((), ())), preferred_element_type=jnp.float32,
            )
            total = now if total is None else total + now
        out[low:low + MTILE, :] = (total * scale).astype(out.dtype)


def products(where, acts, pieces, total, dtype, scale=1.0):
    rows = acts.shape[1]
    vmem = pl.BlockSpec(memory_space=pltpu.VMEM)
    arrays = [acts] + [p.reshape(rows, TC) for p in pieces] + ([] if total is None else [total])
    return pl.pallas_call(
        lambda *refs: product_kernel(len(pieces), scale, total is not None, *refs),
        in_specs=[pl.BlockSpec(memory_space=pltpu.SMEM)] + [vmem] * len(arrays),
        out_specs=vmem,
        out_shape=jax.ShapeDtypeStruct((TR, TC), dtype),
        cost_estimate=pl.CostEstimate(
            flops=2 * len(pieces) * rows * TR * TC,
            bytes_accessed=len(pieces) * rows * (TR + TC) * 2 + 4 * TR * TC, transcendentals=0,
        ),
        compiler_params=pltpu.CompilerParams(vmem_limit_bytes=40 << 20),
    )(where, *arrays)


def gather_and_multiply(cap, recv, aidx, gidx, count, total, dtype, scale):
    y, zh, core = lax.axis_index("y"), lax.axis_index("zh"), lax.axis_index("core")
    acts_c, grads_c = compact(cap, recv, aidx, gidx, count)
    near = lax.ppermute(grads_c, "x", ring("x", NX, -1))
    plane = [(z, c) for z in range(NZ) for c in range(2)]
    hop = [((z * 2 + c), (z + (2 if c == 0 else -2)) % NZ * 2 + c) for z, c in plane]
    far = lax.ppermute(grads_c, ("zh", "zl", "core"), hop)
    far, near, acts_c = lax.optimization_barrier((far, near, acts_c))
    far = lax.ppermute(
        far, ("x", "zh", "zl", "core"),
        [(s * 2 * NZ + i, (s - 1) % NX * 2 * NZ + j) for s in range(NX) for i, j in hop],
    )
    acts_all = lax.all_gather(acts_c, ("zl", "core")).reshape(DGRID, cap * SUB, TR)

    def beside(own):
        up = lax.ppermute(own, "y", ring("y", NY, 1))
        down = lax.ppermute(own, "y", ring("y", NY, -1))
        return up, down

    def across(up, down):
        way = [(yy * 2 + c, (yy + (1 if c == 0 else -1)) % NY * 2 + c) for yy in range(NY) for c in range(2)]
        pairs = [(i // 2 * 2 * NZ + i % 2, j // 2 * 2 * NZ + j % 2) for i, j in way]
        pairs = [(i + 2 * z, j + 2 * z) for z in range(NZ) for i, j in pairs]
        return lax.ppermute(jnp.where(core == 0, up, down), DP, pairs)

    def places(flip):
        h = 1 - zh if flip else zh
        return jnp.stack([lax.rem(y + NY - d, NY) * 2 + h for d in (0, 1, 3, 2)]).astype(jnp.int32)

    up, down = beside(near)
    third = across(up, down)
    far_up, far_down = beside(far)
    far_third = across(far_up, far_down)
    here, there = places(False), places(True)
    total = products(here[:3], acts_all, (near, up, down), total, jnp.float32)
    both = jnp.concatenate([here[3:], there[:3]])
    total = products(both, acts_all, (third, far, far_up, far_down), total, jnp.float32)
    return products(there[3:], acts_all, (far_third,), total, dtype, scale)


def shards(acts, grad_rows, block_experts):
    packed = pack(acts[0], grad_rows[0])
    behind = [block_experts] + [
        lax.ppermute(block_experts, "x", ring("x", NX, d)) for d in (1, 2, 3)
    ]
    touched = [jnp.any(b[0] == 0, axis=1) for b in behind]
    counts = [jnp.sum(t.astype(jnp.int32)) for t in touched]
    most = jnp.maximum(jnp.maximum(counts[0], counts[1]), jnp.maximum(counts[2], counts[3]))
    aidx, gidx = order_of(touched[0]), order_of(touched[1])
    recv = lax.all_to_all(packed, DP, split_axis=0, concat_axis=0, tiled=True)

    scale = 2.0 / math.sqrt(BLOCKS * BLOCK)

    def straight(cap):
        def run(recv, aidx, gidx, count, most):
            return gather_and_multiply(
                cap, recv, aidx[:cap], gidx[:cap], jnp.minimum(count, cap), None, jnp.bfloat16, scale
            )
        return run

    def rounds(recv, aidx, gidx, count, most):
        def one(j, total):
            start = j * MORE
            return gather_and_multiply(
                MORE, recv,
                lax.dynamic_slice_in_dim(aidx, start, MORE),
                lax.dynamic_slice_in_dim(gidx, start, MORE),
                jnp.clip(count - start, 0, MORE), total, jnp.float32, 1.0,
            )

        turns = (most + MORE - 1) // MORE
        total = lax.fori_loop(0, turns, one, jnp.zeros((TR, TC), jnp.float32))
        return (total * scale).astype(jnp.bfloat16)

    which = jnp.sum(most <= jnp.array(CAPS, jnp.int32)).astype(jnp.int32)
    out = lax.switch(
        which, [rounds] + [straight(cap) for cap in CAPS],
        recv, aidx, gidx, counts[0].reshape(1), most,
    )
    return out[None, None]


def solution(mesh):
    fine = Mesh(mesh.devices.reshape(NX, NY, 2, 4, 2), ("x",) + DP)
    return jax.shard_map(
        shards,
        mesh=fine,
        in_specs=(P("x", DP, None), P("x", DP, None), P("x", None, None)),
        out_specs=P("x", DP, None, None),
        check_vma=False,
    )
```

```python
import math

import jax
import jax.numpy as jnp
from jax import lax
from jax.experimental import pallas as pl
from jax.experimental.pallas import tpu as pltpu
from jax.sharding import Mesh
from jax.sharding import PartitionSpec as P

DW = 4096
HW = 8192
BLOCK = 128
DGRID = 8
HGRID = 8
BLOCKS = 64
SUB = BLOCK // DGRID
TR = DW // DGRID
TC = HW // HGRID
NY = 4
NX = 4

NZ = 8
MTILE = 256

CAPS = (24, 20, 18)
MORE = 28
DP = ("y", "zh", "zl", "core")


def pack_kernel(acts_ref, grads_ref, out_ref):
    for a in range(2):
        for c in range(HGRID):
            out_ref[a * HGRID + c, :, :TR] = acts_ref[c * SUB:(c + 1) * SUB, a * TR:(a + 1) * TR]
            out_ref[a * HGRID + c, :, TR:] = grads_ref[a * SUB:(a + 1) * SUB, c * TC:(c + 1) * TC]


def pack(acts, grads):
    return pl.pallas_call(
        pack_kernel,
        grid=(DGRID // 2,),
        in_specs=[
            pl.BlockSpec((BLOCK, 2 * TR), lambda a: (0, a)),
            pl.BlockSpec((2 * SUB, HW), lambda a: (a, 0)),
        ],
        out_specs=pl.BlockSpec((2 * HGRID, SUB, TR + TC), lambda a: (a, 0, 0)),
        out_shape=jax.ShapeDtypeStruct((DGRID * HGRID, SUB, TR + TC), jnp.bfloat16),
    )(acts, grads)


def compact_kernel(cap, aidx, gidx, count, recv, acts_out, grads_out, asem, gsem):
    def acopy(k):
        return pltpu.make_async_copy(recv.at[aidx[k], :, pl.ds(0, TR)], acts_out.at[k], asem.at[k])

    def gcopy(k):
        return pltpu.make_async_copy(recv.at[gidx[k], :, pl.ds(TR, TC)], grads_out.at[k], gsem.at[k])

    def start(k, carry):
        gcopy(k).start()
        acopy(k).start()
        return carry

    def finish(k, carry):
        gcopy(k).wait()
        acopy(k).wait()
        return carry

    lax.fori_loop(0, cap, start, 0)
    lax.fori_loop(0, cap, finish, 0)

    def clear(k, carry):
        acts_out[k] = jnp.zeros((SUB, TR), jnp.bfloat16)
        return carry

    lax.fori_loop(count[0], cap, clear, 0)


def compact(cap, recv, aidx, gidx, count):
    smem = pl.BlockSpec(memory_space=pltpu.SMEM)
    vmem = pl.BlockSpec(memory_space=pltpu.VMEM)
    return pl.pallas_call(
        lambda *refs: compact_kernel(cap, *refs),
        in_specs=[smem, smem, smem, pl.BlockSpec(memory_space=pl.ANY)],
        out_specs=[vmem, vmem],
        out_shape=[
            jax.ShapeDtypeStruct((cap, SUB, TR), jnp.bfloat16),
            jax.ShapeDtypeStruct((cap, SUB, TC), jnp.bfloat16),
        ],
        scratch_shapes=[pltpu.SemaphoreType.DMA((cap,)), pltpu.SemaphoreType.DMA((cap,))],
    )(aidx, gidx, count, recv)


def order_of(touched):
    blocks = jnp.arange(BLOCKS)
    rank = jnp.sum((blocks[None, :] < blocks[:, None]) & touched[None, :], axis=1)
    hit = touched[None, :] & (rank[None, :] == blocks[:, None])
    return jnp.sum(jnp.where(hit, blocks[None, :], 0), axis=1).astype(jnp.int32)


def ring(axis, size, distance):
    return [(i, (i + distance) % size) for i in range(size)]


def product_kernel(n, scale, has_total, *refs):
    where, acts = refs[0], refs[1]
    pieces, rest = refs[2:2 + n], refs[2 + n:]
    out = rest[-1]

    def tile(t, carry):
        rows = pl.ds(pl.multiple_of(t * MTILE, MTILE), MTILE)
        total = rest[0][rows, :] if has_total else None
        for i in range(n):
            now = lax.dot_general(
                acts[where[i], :, rows], pieces[i][...],
                (((0,), (0,)), ((), ())), preferred_element_type=jnp.float32,
            )
            total = now if total is None else total + now
        out[rows, :] = (total * scale).astype(out.dtype)
        return carry

    lax.fori_loop(0, TR // MTILE, tile, 0)


def products(where, acts, pieces, total, dtype, scale=1.0):
    rows = acts.shape[1]
    vmem = pl.BlockSpec(memory_space=pltpu.VMEM)
    arrays = [acts] + [p.reshape(rows, TC) for p in pieces] + ([] if total is None else [total])
    return pl.pallas_call(
        lambda *refs: product_kernel(len(pieces), scale, total is not None, *refs),
        in_specs=[pl.BlockSpec(memory_space=pltpu.SMEM)] + [vmem] * len(arrays),
        out_specs=vmem,
        out_shape=jax.ShapeDtypeStruct((TR, TC), dtype),
        cost_estimate=pl.CostEstimate(
            flops=2 * len(pieces) * rows * TR * TC,
            bytes_accessed=len(pieces) * rows * (TR + TC) * 2 + 4 * TR * TC, transcendentals=0,
        ),
        compiler_params=pltpu.CompilerParams(vmem_limit_bytes=40 << 20),
    )(where, *arrays)


def gather_and_multiply(cap, recv, aidx, gidx, count, total, dtype, scale):
    y, zh, core = lax.axis_index("y"), lax.axis_index("zh"), lax.axis_index("core")
    acts_c, grads_c = compact(cap, recv, aidx, gidx, count)
    near = lax.ppermute(grads_c, "x", ring("x", NX, -1))
    plane = [(z, c) for z in range(NZ) for c in range(2)]
    hop = [((z * 2 + c), (z + (2 if c == 0 else -2)) % NZ * 2 + c) for z, c in plane]
    far = lax.ppermute(grads_c, ("zh", "zl", "core"), hop)
    far, near, acts_c = lax.optimization_barrier((far, near, acts_c))
    far = lax.ppermute(
        far, ("x", "zh", "zl", "core"),
        [(s * 2 * NZ + i, (s - 1) % NX * 2 * NZ + j) for s in range(NX) for i, j in hop],
    )
    acts_all = lax.all_gather(acts_c, ("zl", "core")).reshape(DGRID, cap * SUB, TR)

    def beside(own):
        up = lax.ppermute(own, "y", ring("y", NY, 1))
        down = lax.ppermute(own, "y", ring("y", NY, -1))
        return up, down

    def across(up, down):
        way = [(yy * 2 + c, (yy + (1 if c == 0 else -1)) % NY * 2 + c) for yy in range(NY) for c in range(2)]
        pairs = [(i // 2 * 2 * NZ + i % 2, j // 2 * 2 * NZ + j % 2) for i, j in way]
        pairs = [(i + 2 * z, j + 2 * z) for z in range(NZ) for i, j in pairs]
        return lax.ppermute(jnp.where(core == 0, up, down), DP, pairs)

    def places(flip):
        h = 1 - zh if flip else zh
        return jnp.stack([lax.rem(y + NY - d, NY) * 2 + h for d in (0, 1, 3, 2)]).astype(jnp.int32)

    up, down = beside(near)
    third = across(up, down)
    far_up, far_down = beside(far)
    far_third = across(far_up, far_down)
    here, there = places(False), places(True)
    total = products(here[:3], acts_all, (near, up, down), total, jnp.float32)
    both = jnp.concatenate([here[3:], there[:3]])
    total = products(both, acts_all, (third, far, far_up, far_down), total, jnp.float32)
    return products(there[3:], acts_all, (far_third,), total, dtype, scale)


def shards(acts, grad_rows, block_experts):
    packed = pack(acts[0], grad_rows[0])
    behind = [block_experts] + [
        lax.ppermute(block_experts, "x", ring("x", NX, d)) for d in (1, 2, 3)
    ]
    touched = [jnp.any(b[0] == 0, axis=1) for b in behind]
    counts = [jnp.sum(t.astype(jnp.int32)) for t in touched]
    most = jnp.maximum(jnp.maximum(counts[0], counts[1]), jnp.maximum(counts[2], counts[3]))
    aidx, gidx = order_of(touched[0]), order_of(touched[1])
    recv = lax.all_to_all(packed, DP, split_axis=0, concat_axis=0, tiled=True)

    scale = 2.0 / math.sqrt(BLOCKS * BLOCK)

    def straight(cap):
        def run(recv, aidx, gidx, count, most):
            return gather_and_multiply(
                cap, recv, aidx[:cap], gidx[:cap], jnp.minimum(count, cap), None, jnp.bfloat16, scale
            )
        return run

    def rounds(recv, aidx, gidx, count, most):
        def one(j, total):
            start = j * MORE
            return gather_and_multiply(
                MORE, recv,
                lax.dynamic_slice_in_dim(aidx, start, MORE),
                lax.dynamic_slice_in_dim(gidx, start, MORE),
                jnp.clip(count - start, 0, MORE), total, jnp.float32, 1.0,
            )

        turns = (most + MORE - 1) // MORE
        total = lax.fori_loop(0, turns, one, jnp.zeros((TR, TC), jnp.float32))
        return (total * scale).astype(jnp.bfloat16)

    which = jnp.sum(most <= jnp.array(CAPS, jnp.int32)).astype(jnp.int32)
    out = lax.switch(
        which, [rounds] + [straight(cap) for cap in CAPS],
        recv, aidx, gidx, counts[0].reshape(1), most,
    )
    return out[None, None]


def solution(mesh):
    fine = Mesh(mesh.devices.reshape(NX, NY, 2, 4, 2), ("x",) + DP)
    return jax.shard_map(
        shards,
        mesh=fine,
        in_specs=(P("x", DP, None), P("x", DP, None), P("x", None, None)),
        out_specs=P("x", DP, None, None),
        check_vma=False,
    )
```

```python
import math

import jax
import jax.numpy as jnp
from jax import lax
from jax.experimental import pallas as pl
from jax.experimental.pallas import tpu as pltpu
from jax.sharding import Mesh
from jax.sharding import PartitionSpec as P

DW = 4096
HW = 8192
BLOCK = 128
DGRID = 8
HGRID = 8
BLOCKS = 64
SUB = BLOCK // DGRID
TR = DW // DGRID
TC = HW // HGRID
NY = 4
NX = 4

NZ = 8
MTILE = 256

MAIN = 20
MORE = 28
DP = ("y", "zh", "zl", "core")


def pack_kernel(acts_ref, grads_ref, out_ref):
    for a in range(2):
        for c in range(HGRID):
            out_ref[a * HGRID + c, :, :TR] = acts_ref[c * SUB:(c + 1) * SUB, a * TR:(a + 1) * TR]
            out_ref[a * HGRID + c, :, TR:] = grads_ref[a * SUB:(a + 1) * SUB, c * TC:(c + 1) * TC]


def pack(acts, grads):
    return pl.pallas_call(
        pack_kernel,
        grid=(DGRID // 2,),
        in_specs=[
            pl.BlockSpec((BLOCK, 2 * TR), lambda a: (0, a)),
            pl.BlockSpec((2 * SUB, HW), lambda a: (a, 0)),
        ],
        out_specs=pl.BlockSpec((2 * HGRID, SUB, TR + TC), lambda a: (a, 0, 0)),
        out_shape=jax.ShapeDtypeStruct((DGRID * HGRID, SUB, TR + TC), jnp.bfloat16),
    )(acts, grads)


def compact_kernel(cap, aidx, gidx, count, recv, acts_out, grads_out, asem, gsem):
    def acopy(k):
        return pltpu.make_async_copy(recv.at[aidx[k], :, pl.ds(0, TR)], acts_out.at[k], asem.at[k])

    def gcopy(k):
        return pltpu.make_async_copy(recv.at[gidx[k], :, pl.ds(TR, TC)], grads_out.at[k], gsem.at[k])

    def start(k, carry):
        gcopy(k).start()
        acopy(k).start()
        return carry

    def finish(k, carry):
        gcopy(k).wait()
        acopy(k).wait()
        return carry

    lax.fori_loop(0, cap, start, 0)
    lax.fori_loop(0, cap, finish, 0)

    def clear(k, carry):
        acts_out[k] = jnp.zeros((SUB, TR), jnp.bfloat16)
        return carry

    lax.fori_loop(count[0], cap, clear, 0)


def compact(cap, recv, aidx, gidx, count):
    smem = pl.BlockSpec(memory_space=pltpu.SMEM)
    vmem = pl.BlockSpec(memory_space=pltpu.VMEM)
    return pl.pallas_call(
        lambda *refs: compact_kernel(cap, *refs),
        in_specs=[smem, smem, smem, pl.BlockSpec(memory_space=pl.ANY)],
        out_specs=[vmem, vmem],
        out_shape=[
            jax.ShapeDtypeStruct((cap, SUB, TR), jnp.bfloat16),
            jax.ShapeDtypeStruct((cap, SUB, TC), jnp.bfloat16),
        ],
        scratch_shapes=[pltpu.SemaphoreType.DMA((cap,)), pltpu.SemaphoreType.DMA((cap,))],
    )(aidx, gidx, count, recv)


def order_of(touched):
    blocks = jnp.arange(BLOCKS)
    rank = jnp.sum((blocks[None, :] < blocks[:, None]) & touched[None, :], axis=1)
    hit = touched[None, :] & (rank[None, :] == blocks[:, None])
    return jnp.sum(jnp.where(hit, blocks[None, :], 0), axis=1).astype(jnp.int32)


def ring(axis, size, distance):
    return [(i, (i + distance) % size) for i in range(size)]


def product_kernel(n, scale, has_total, *refs):
    where, acts = refs[0], refs[1]
    pieces, rest = refs[2:2 + n], refs[2 + n:]
    out = rest[-1]

    def tile(t, carry):
        rows = pl.ds(pl.multiple_of(t * MTILE, MTILE), MTILE)
        total = rest[0][rows, :] if has_total else None
        for i in range(n):
            now = lax.dot_general(
                acts[where[i], :, rows], pieces[i][...],
                (((0,), (0,)), ((), ())), preferred_element_type=jnp.float32,
            )
            total = now if total is None else total + now
        out[rows, :] = (total * scale).astype(out.dtype)
        return carry

    lax.fori_loop(0, TR // MTILE, tile, 0)


def products(where, acts, pieces, total, dtype, scale=1.0):
    rows = acts.shape[1]
    vmem = pl.BlockSpec(memory_space=pltpu.VMEM)
    arrays = [acts] + [p.reshape(rows, TC) for p in pieces] + ([] if total is None else [total])
    return pl.pallas_call(
        lambda *refs: product_kernel(len(pieces), scale, total is not None, *refs),
        in_specs=[pl.BlockSpec(memory_space=pltpu.SMEM)] + [vmem] * len(arrays),
        out_specs=vmem,
        out_shape=jax.ShapeDtypeStruct((TR, TC), dtype),
        cost_estimate=pl.CostEstimate(
            flops=2 * len(pieces) * rows * TR * TC,
            bytes_accessed=len(pieces) * rows * (TR + TC) * 2 + 4 * TR * TC, transcendentals=0,
        ),
        compiler_params=pltpu.CompilerParams(vmem_limit_bytes=40 << 20),
    )(where, *arrays)


def gather_and_multiply(cap, recv, aidx, gidx, count, total, dtype, scale):
    y, zh, core = lax.axis_index("y"), lax.axis_index("zh"), lax.axis_index("core")
    acts_c, grads_c = compact(cap, recv, aidx, gidx, count)
    near = lax.ppermute(grads_c, "x", ring("x", NX, -1))
    plane = [(z, c) for z in range(NZ) for c in range(2)]
    hop = [((z * 2 + c), (z + (2 if c == 0 else -2)) % NZ * 2 + c) for z, c in plane]
    far = lax.ppermute(grads_c, ("zh", "zl", "core"), hop)
    far, near, acts_c = lax.optimization_barrier((far, near, acts_c))
    far = lax.ppermute(
        far, ("x", "zh", "zl", "core"),
        [(s * 2 * NZ + i, (s - 1) % NX * 2 * NZ + j) for s in range(NX) for i, j in hop],
    )
    acts_all = lax.all_gather(acts_c, ("zl", "core")).reshape(DGRID, cap * SUB, TR)

    def beside(own):
        up = lax.ppermute(own, "y", ring("y", NY, 1))
        down = lax.ppermute(own, "y", ring("y", NY, -1))
        return up, down

    def across(up, down):
        way = [(yy * 2 + c, (yy + (1 if c == 0 else -1)) % NY * 2 + c) for yy in range(NY) for c in range(2)]
        pairs = [(i // 2 * 2 * NZ + i % 2, j // 2 * 2 * NZ + j % 2) for i, j in way]
        pairs = [(i + 2 * z, j + 2 * z) for z in range(NZ) for i, j in pairs]
        return lax.ppermute(jnp.where(core == 0, up, down), DP, pairs)

    def places(flip):
        h = 1 - zh if flip else zh
        return jnp.stack([lax.rem(y + NY - d, NY) * 2 + h for d in (0, 1, 3, 2)]).astype(jnp.int32)

    up, down = beside(near)
    third = across(up, down)
    far_up, far_down = beside(far)
    far_third = across(far_up, far_down)
    here, there = places(False), places(True)
    total = products(here[:3], acts_all, (near, up, down), total, jnp.float32)
    both = jnp.concatenate([here[3:], there[:3]])
    total = products(both, acts_all, (third, far, far_up, far_down), total, jnp.float32)
    return products(there[3:], acts_all, (far_third,), total, dtype, scale)


def shards(acts, grad_rows, block_experts):
    packed = pack(acts[0], grad_rows[0])
    behind = [block_experts] + [
        lax.ppermute(block_experts, "x", ring("x", NX, d)) for d in (1, 2, 3)
    ]
    touched = [jnp.any(b[0] == 0, axis=1) for b in behind]
    counts = [jnp.sum(t.astype(jnp.int32)) for t in touched]
    most = jnp.maximum(jnp.maximum(counts[0], counts[1]), jnp.maximum(counts[2], counts[3]))
    aidx, gidx = order_of(touched[0]), order_of(touched[1])
    recv = lax.all_to_all(packed, DP, split_axis=0, concat_axis=0, tiled=True)

    scale = 2.0 / math.sqrt(BLOCKS * BLOCK)

    def straight(cap):
        def run(recv, aidx, gidx, count, most):
            return gather_and_multiply(
                cap, recv, aidx[:cap], gidx[:cap], jnp.minimum(count, cap), None, jnp.bfloat16, scale
            )
        return run

    def rounds(recv, aidx, gidx, count, most):
        def one(j, total):
            start = j * MORE
            return gather_and_multiply(
                MORE, recv,
                lax.dynamic_slice_in_dim(aidx, start, MORE),
                lax.dynamic_slice_in_dim(gidx, start, MORE),
                jnp.clip(count - start, 0, MORE), total, jnp.float32, 1.0,
            )

        turns = (most + MORE - 1) // MORE
        total = lax.fori_loop(0, turns, one, jnp.zeros((TR, TC), jnp.float32))
        return (total * scale).astype(jnp.bfloat16)

    out = lax.switch(
        (most > MAIN).astype(jnp.int32), [straight(MAIN), rounds],
        recv, aidx, gidx, counts[0].reshape(1), most,
    )
    return out[None, None]


def solution(mesh):
    fine = Mesh(mesh.devices.reshape(NX, NY, 2, 4, 2), ("x",) + DP)
    return jax.shard_map(
        shards,
        mesh=fine,
        in_specs=(P("x", DP, None), P("x", DP, None), P("x", None, None)),
        out_specs=P("x", DP, None, None),
        check_vma=False,
    )
```

```python
import math

import jax
import jax.numpy as jnp
from jax import lax
from jax.experimental import pallas as pl
from jax.experimental.pallas import tpu as pltpu
from jax.sharding import Mesh
from jax.sharding import PartitionSpec as P

DW = 4096
HW = 8192
BLOCK = 128
DGRID = 8
HGRID = 8
BLOCKS = 64
SUB = BLOCK // DGRID
TR = DW // DGRID
TC = HW // HGRID
NY = 4
NX = 4

NZ = 8
MTILE = 256

MAIN = 20
MORE = 28
DP = ("y", "zh", "zl", "core")


def pack_kernel(acts_ref, grads_ref, out_ref):
    for a in range(4):
        for c in range(HGRID):
            out_ref[a * HGRID + c, :, :TR] = acts_ref[c * SUB:(c + 1) * SUB, a * TR:(a + 1) * TR]
            out_ref[a * HGRID + c, :, TR:] = grads_ref[a * SUB:(a + 1) * SUB, c * TC:(c + 1) * TC]


def pack(acts, grads):
    return pl.pallas_call(
        pack_kernel,
        grid=(DGRID // 4,),
        in_specs=[
            pl.BlockSpec((BLOCK, 4 * TR), lambda a: (0, a)),
            pl.BlockSpec((4 * SUB, HW), lambda a: (a, 0)),
        ],
        out_specs=pl.BlockSpec((4 * HGRID, SUB, TR + TC), lambda a: (a, 0, 0)),
        out_shape=jax.ShapeDtypeStruct((DGRID * HGRID, SUB, TR + TC), jnp.bfloat16),
    )(acts, grads)


def compact_kernel(cap, aidx, gidx, count, recv, acts_out, grads_out, asem, gsem):
    def acopy(k):
        return pltpu.make_async_copy(recv.at[aidx[k], :, pl.ds(0, TR)], acts_out.at[k], asem.at[k])

    def gcopy(k):
        return pltpu.make_async_copy(recv.at[gidx[k], :, pl.ds(TR, TC)], grads_out.at[k], gsem.at[k])

    def start(k, carry):
        gcopy(k).start()
        acopy(k).start()
        return carry

    def finish(k, carry):
        gcopy(k).wait()
        acopy(k).wait()
        return carry

    lax.fori_loop(0, cap, start, 0)
    lax.fori_loop(0, cap, finish, 0)

    def clear(k, carry):
        acts_out[k] = jnp.zeros((SUB, TR), jnp.bfloat16)
        return carry

    lax.fori_loop(count[0], cap, clear, 0)


def compact(cap, recv, aidx, gidx, count):
    smem = pl.BlockSpec(memory_space=pltpu.SMEM)
    vmem = pl.BlockSpec(memory_space=pltpu.VMEM)
    return pl.pallas_call(
        lambda *refs: compact_kernel(cap, *refs),
        in_specs=[smem, smem, smem, pl.BlockSpec(memory_space=pl.ANY)],
        out_specs=[vmem, vmem],
        out_shape=[
            jax.ShapeDtypeStruct((cap, SUB, TR), jnp.bfloat16),
            jax.ShapeDtypeStruct((cap, SUB, TC), jnp.bfloat16),
        ],
        scratch_shapes=[pltpu.SemaphoreType.DMA((cap,)), pltpu.SemaphoreType.DMA((cap,))],
    )(aidx, gidx, count, recv)


def order_of(touched):
    blocks = jnp.arange(BLOCKS)
    rank = jnp.sum((blocks[None, :] < blocks[:, None]) & touched[None, :], axis=1)
    hit = touched[None, :] & (rank[None, :] == blocks[:, None])
    return jnp.sum(jnp.where(hit, blocks[None, :], 0), axis=1).astype(jnp.int32)


def ring(axis, size, distance):
    return [(i, (i + distance) % size) for i in range(size)]


def product_kernel(n, scale, has_total, *refs):
    where, acts = refs[0], refs[1]
    pieces, rest = refs[2:2 + n], refs[2 + n:]
    out = rest[-1]

    def tile(t, carry):
        rows = pl.ds(pl.multiple_of(t * MTILE, MTILE), MTILE)
        total = rest[0][rows, :] if has_total else None
        for i in range(n):
            now = lax.dot_general(
                acts[where[i], :, rows], pieces[i][...],
                (((0,), (0,)), ((), ())), preferred_element_type=jnp.float32,
            )
            total = now if total is None else total + now
        out[rows, :] = (total * scale).astype(out.dtype)
        return carry

    lax.fori_loop(0, TR // MTILE, tile, 0)


def products(where, acts, pieces, total, dtype, scale=1.0):
    rows = acts.shape[1]
    vmem = pl.BlockSpec(memory_space=pltpu.VMEM)
    arrays = [acts] + [p.reshape(rows, TC) for p in pieces] + ([] if total is None else [total])
    return pl.pallas_call(
        lambda *refs: product_kernel(len(pieces), scale, total is not None, *refs),
        in_specs=[pl.BlockSpec(memory_space=pltpu.SMEM)] + [vmem] * len(arrays),
        out_specs=vmem,
        out_shape=jax.ShapeDtypeStruct((TR, TC), dtype),
        cost_estimate=pl.CostEstimate(
            flops=2 * len(pieces) * rows * TR * TC,
            bytes_accessed=len(pieces) * rows * (TR + TC) * 2 + 4 * TR * TC, transcendentals=0,
        ),
        compiler_params=pltpu.CompilerParams(vmem_limit_bytes=40 << 20),
    )(where, *arrays)


def gather_and_multiply(cap, recv, aidx, gidx, count, total, dtype, scale):
    y, zh, core = lax.axis_index("y"), lax.axis_index("zh"), lax.axis_index("core")
    acts_c, grads_c = compact(cap, recv, aidx, gidx, count)
    plane = [(z, c) for z in range(NZ) for c in range(2)]
    hop = [((z * 2 + c), (z + (2 if c == 0 else -2)) % NZ * 2 + c) for z, c in plane]
    far = lax.ppermute(grads_c, ("zh", "zl", "core"), hop)
    near = lax.ppermute(grads_c, "x", ring("x", NX, -1))
    far, near, acts_c = lax.optimization_barrier((far, near, acts_c))
    far = lax.ppermute(
        far, ("x", "zh", "zl", "core"),
        [(s * 2 * NZ + i, (s - 1) % NX * 2 * NZ + j) for s in range(NX) for i, j in hop],
    )
    acts_all = lax.all_gather(acts_c, ("zl", "core")).reshape(DGRID, cap * SUB, TR)

    def beside(own):
        up = lax.ppermute(own, "y", ring("y", NY, 1))
        down = lax.ppermute(own, "y", ring("y", NY, -1))
        return up, down

    def across(up, down):
        way = [(yy * 2 + c, (yy + (1 if c == 0 else -1)) % NY * 2 + c) for yy in range(NY) for c in range(2)]
        pairs = [(i // 2 * 2 * NZ + i % 2, j // 2 * 2 * NZ + j % 2) for i, j in way]
        pairs = [(i + 2 * z, j + 2 * z) for z in range(NZ) for i, j in pairs]
        return lax.ppermute(jnp.where(core == 0, up, down), DP, pairs)

    def places(flip):
        h = 1 - zh if flip else zh
        return jnp.stack([lax.rem(y + NY - d, NY) * 2 + h for d in (0, 1, 3, 2)]).astype(jnp.int32)

    up, down = beside(near)
    third = across(up, down)
    far_up, far_down = beside(far)
    far_third = across(far_up, far_down)
    here, there = places(False), places(True)
    total = products(here[:3], acts_all, (near, up, down), total, jnp.float32)
    both = jnp.concatenate([here[3:], there[:3]])
    total = products(both, acts_all, (third, far, far_up, far_down), total, jnp.float32)
    return products(there[3:], acts_all, (far_third,), total, dtype, scale)


def shards(acts, grad_rows, block_experts):
    packed = pack(acts[0], grad_rows[0])
    behind = [block_experts] + [
        lax.ppermute(block_experts, "x", ring("x", NX, d)) for d in (1, 2, 3)
    ]
    touched = [jnp.any(b[0] == 0, axis=1) for b in behind]
    counts = [jnp.sum(t.astype(jnp.int32)) for t in touched]
    most = jnp.maximum(jnp.maximum(counts[0], counts[1]), jnp.maximum(counts[2], counts[3]))
    aidx, gidx = (jnp.pad(order_of(t), (0, MORE)) for t in touched[:2])
    recv = lax.all_to_all(packed, DP, split_axis=0, concat_axis=0, tiled=True)

    scale = 2.0 / math.sqrt(BLOCKS * BLOCK)

    def straight(cap):
        def run(recv, aidx, gidx, count, most):
            return gather_and_multiply(
                cap, recv, aidx[:cap], gidx[:cap], jnp.minimum(count, cap), None, jnp.bfloat16, scale
            )
        return run

    def rounds(recv, aidx, gidx, count, most):
        def one(j, total):
            start = j * MORE
            return gather_and_multiply(
                MORE, recv,
                lax.dynamic_slice_in_dim(aidx, start, MORE),
                lax.dynamic_slice_in_dim(gidx, start, MORE),
                jnp.clip(count - start, 0, MORE), total, jnp.float32, 1.0,
            )

        turns = (most + MORE - 1) // MORE
        total = lax.fori_loop(0, turns, one, jnp.zeros((TR, TC), jnp.float32))
        return (total * scale).astype(jnp.bfloat16)

    out = lax.switch(
        (most > MAIN).astype(jnp.int32), [straight(MAIN), rounds],
        recv, aidx, gidx, counts[0].reshape(1), most,
    )
    return out[None, None]


def solution(mesh):
    fine = Mesh(mesh.devices.reshape(NX, NY, 2, 4, 2), ("x",) + DP)
    return jax.shard_map(
        shards,
        mesh=fine,
        in_specs=(P("x", DP, None), P("x", DP, None), P("x", None, None)),
        out_specs=P("x", DP, None, None),
        check_vma=False,
    )
```

```python
import math

import jax
import jax.numpy as jnp
from jax import lax
from jax.experimental import pallas as pl
from jax.experimental.pallas import tpu as pltpu
from jax.sharding import Mesh
from jax.sharding import PartitionSpec as P

DW = 4096
HW = 8192
BLOCK = 128
DGRID = 8
HGRID = 8
BLOCKS = 64
SUB = BLOCK // DGRID
TR = DW // DGRID
TC = HW // HGRID
NY = 4
NX = 4

NZ = 8
MTILE = 256

MAIN = 20
MORE = 32
DP = ("y", "zh", "zl", "core")


def pack_kernel(acts_ref, grads_ref, out_ref):
    for a in range(4):
        for c in range(HGRID):
            out_ref[a * HGRID + c, :, :TR] = acts_ref[c * SUB:(c + 1) * SUB, a * TR:(a + 1) * TR]
            out_ref[a * HGRID + c, :, TR:] = grads_ref[a * SUB:(a + 1) * SUB, c * TC:(c + 1) * TC]


def pack(acts, grads):
    return pl.pallas_call(
        pack_kernel,
        grid=(DGRID // 4,),
        in_specs=[
            pl.BlockSpec((BLOCK, 4 * TR), lambda a: (0, a)),
            pl.BlockSpec((4 * SUB, HW), lambda a: (a, 0)),
        ],
        out_specs=pl.BlockSpec((4 * HGRID, SUB, TR + TC), lambda a: (a, 0, 0)),
        out_shape=jax.ShapeDtypeStruct((DGRID * HGRID, SUB, TR + TC), jnp.bfloat16),
    )(acts, grads)


def compact_kernel(cap, aidx, gidx, count, recv, acts_out, grads_out, asem, gsem):
    def acopy(k):
        return pltpu.make_async_copy(recv.at[aidx[k], :, pl.ds(0, TR)], acts_out.at[k], asem.at[k])

    def gcopy(k):
        return pltpu.make_async_copy(recv.at[gidx[k], :, pl.ds(TR, TC)], grads_out.at[k], gsem.at[k])

    def start(k, carry):
        gcopy(k).start()
        acopy(k).start()
        return carry

    def finish(k, carry):
        gcopy(k).wait()
        acopy(k).wait()
        return carry

    lax.fori_loop(0, cap, start, 0)
    lax.fori_loop(0, cap, finish, 0)

    def clear(k, carry):
        acts_out[k] = jnp.zeros((SUB, TR), jnp.bfloat16)
        return carry

    lax.fori_loop(count[0], cap, clear, 0)


def compact(cap, recv, aidx, gidx, count):
    smem = pl.BlockSpec(memory_space=pltpu.SMEM)
    vmem = pl.BlockSpec(memory_space=pltpu.VMEM)
    return pl.pallas_call(
        lambda *refs: compact_kernel(cap, *refs),
        in_specs=[smem, smem, smem, pl.BlockSpec(memory_space=pl.ANY)],
        out_specs=[vmem, vmem],
        out_shape=[
            jax.ShapeDtypeStruct((cap, SUB, TR), jnp.bfloat16),
            jax.ShapeDtypeStruct((cap, SUB, TC), jnp.bfloat16),
        ],
        scratch_shapes=[pltpu.SemaphoreType.DMA((cap,)), pltpu.SemaphoreType.DMA((cap,))],
    )(aidx, gidx, count, recv)


def order_of(touched):
    blocks = jnp.arange(BLOCKS)
    rank = jnp.sum((blocks[None, :] < blocks[:, None]) & touched[None, :], axis=1)
    hit = touched[None, :] & (rank[None, :] == blocks[:, None])
    return jnp.sum(jnp.where(hit, blocks[None, :], 0), axis=1).astype(jnp.int32)


def ring(axis, size, distance):
    return [(i, (i + distance) % size) for i in range(size)]


def product_kernel(n, scale, has_total, *refs):
    where, acts = refs[0], refs[1]
    pieces, rest = refs[2:2 + n], refs[2 + n:]
    out = rest[-1]

    def tile(t, carry):
        rows = pl.ds(pl.multiple_of(t * MTILE, MTILE), MTILE)
        total = rest[0][rows, :] if has_total else None
        for i in range(n):
            now = lax.dot_general(
                acts[where[i], :, rows], pieces[i][...],
                (((0,), (0,)), ((), ())), preferred_element_type=jnp.float32,
            )
            total = now if total is None else total + now
        out[rows, :] = (total * scale).astype(out.dtype)
        return carry

    lax.fori_loop(0, TR // MTILE, tile, 0)


def products(where, acts, pieces, total, dtype, scale=1.0):
    rows = acts.shape[1]
    vmem = pl.BlockSpec(memory_space=pltpu.VMEM)
    arrays = [acts] + [p.reshape(rows, TC) for p in pieces] + ([] if total is None else [total])
    return pl.pallas_call(
        lambda *refs: product_kernel(len(pieces), scale, total is not None, *refs),
        in_specs=[pl.BlockSpec(memory_space=pltpu.SMEM)] + [vmem] * len(arrays),
        out_specs=vmem,
        out_shape=jax.ShapeDtypeStruct((TR, TC), dtype),
        cost_estimate=pl.CostEstimate(
            flops=2 * len(pieces) * rows * TR * TC,
            bytes_accessed=len(pieces) * rows * (TR + TC) * 2 + 4 * TR * TC, transcendentals=0,
        ),
        compiler_params=pltpu.CompilerParams(vmem_limit_bytes=40 << 20),
    )(where, *arrays)


def gather_and_multiply(cap, recv, aidx, gidx, count, total, dtype, scale):
    y, zh, core = lax.axis_index("y"), lax.axis_index("zh"), lax.axis_index("core")
    acts_c, grads_c = compact(cap, recv, aidx, gidx, count)
    plane = [(z, c) for z in range(NZ) for c in range(2)]
    hop = [((z * 2 + c), (z + (2 if c == 0 else -2)) % NZ * 2 + c) for z, c in plane]
    far = lax.ppermute(grads_c, ("zh", "zl", "core"), hop)
    near = lax.ppermute(grads_c, "x", ring("x", NX, -1))
    far, near, acts_c = lax.optimization_barrier((far, near, acts_c))
    far = lax.ppermute(
        far, ("x", "zh", "zl", "core"),
        [(s * 2 * NZ + i, (s - 1) % NX * 2 * NZ + j) for s in range(NX) for i, j in hop],
    )
    acts_all = lax.all_gather(acts_c, ("zl", "core")).reshape(DGRID, cap * SUB, TR)

    def beside(own):
        up = lax.ppermute(own, "y", ring("y", NY, 1))
        down = lax.ppermute(own, "y", ring("y", NY, -1))
        return up, down

    def across(up, down):
        way = [(yy * 2 + c, (yy + (1 if c == 0 else -1)) % NY * 2 + c) for yy in range(NY) for c in range(2)]
        pairs = [(i // 2 * 2 * NZ + i % 2, j // 2 * 2 * NZ + j % 2) for i, j in way]
        pairs = [(i + 2 * z, j + 2 * z) for z in range(NZ) for i, j in pairs]
        return lax.ppermute(jnp.where(core == 0, up, down), DP, pairs)

    def places(flip):
        h = 1 - zh if flip else zh
        return jnp.stack([lax.rem(y + NY - d, NY) * 2 + h for d in (0, 1, 3, 2)]).astype(jnp.int32)

    up, down = beside(near)
    third = across(up, down)
    far_up, far_down = beside(far)
    far_third = across(far_up, far_down)
    here, there = places(False), places(True)
    total = products(here[:3], acts_all, (near, up, down), total, jnp.float32)
    both = jnp.concatenate([here[3:], there[:3]])
    total = products(both, acts_all, (third, far, far_up, far_down), total, jnp.float32)
    return products(there[3:], acts_all, (far_third,), total, dtype, scale)


def shards(acts, grad_rows, block_experts):
    packed = pack(acts[0], grad_rows[0])
    behind = [block_experts] + [
        lax.ppermute(block_experts, "x", ring("x", NX, d)) for d in (1, 2, 3)
    ]
    touched = [jnp.any(b[0] == 0, axis=1) for b in behind]
    counts = [jnp.sum(t.astype(jnp.int32)) for t in touched]
    most = jnp.maximum(jnp.maximum(counts[0], counts[1]), jnp.maximum(counts[2], counts[3]))
    aidx, gidx = (jnp.pad(order_of(t), (0, MORE)) for t in touched[:2])
    recv = lax.all_to_all(packed, DP, split_axis=0, concat_axis=0, tiled=True)

    scale = 2.0 / math.sqrt(BLOCKS * BLOCK)

    def straight(cap):
        def run(recv, aidx, gidx, count, most):
            return gather_and_multiply(
                cap, recv, aidx[:cap], gidx[:cap], jnp.minimum(count, cap), None, jnp.bfloat16, scale
            )
        return run

    def rounds(recv, aidx, gidx, count, most):
        def one(j, total):
            start = j * MORE
            return gather_and_multiply(
                MORE, recv,
                lax.dynamic_slice_in_dim(aidx, start, MORE),
                lax.dynamic_slice_in_dim(gidx, start, MORE),
                jnp.clip(count - start, 0, MORE), total, jnp.float32, 1.0,
            )

        turns = (most + MORE - 1) // MORE
        total = lax.fori_loop(0, turns, one, jnp.zeros((TR, TC), jnp.float32))
        return (total * scale).astype(jnp.bfloat16)

    out = lax.switch(
        (most > MAIN).astype(jnp.int32), [straight(MAIN), rounds],
        recv, aidx, gidx, counts[0].reshape(1), most,
    )
    return out[None, None]


def solution(mesh):
    fine = Mesh(mesh.devices.reshape(NX, NY, 2, 4, 2), ("x",) + DP)
    return jax.shard_map(
        shards,
        mesh=fine,
        in_specs=(P("x", DP, None), P("x", DP, None), P("x", None, None)),
        out_specs=P("x", DP, None, None),
        check_vma=False,
    )
```

```python
import math

import jax
import jax.numpy as jnp
from jax import lax
from jax.experimental import pallas as pl
from jax.experimental.pallas import tpu as pltpu
from jax.sharding import Mesh
from jax.sharding import PartitionSpec as P

DW = 4096
HW = 8192
BLOCK = 128
DGRID = 8
HGRID = 8
BLOCKS = 64
SUB = BLOCK // DGRID
TR = DW // DGRID
TC = HW // HGRID
NY = 4
NX = 4

NZ = 8
MTILE = 256

MAIN = 20
MORE = 32
DP = ("y", "zh", "zl", "core")


def pack_kernel(acts_ref, grads_ref, out_ref):
    for a in range(4):
        for c in range(HGRID):
            out_ref[a * HGRID + c, :, :TR] = acts_ref[c * SUB:(c + 1) * SUB, a * TR:(a + 1) * TR]
            out_ref[a * HGRID + c, :, TR:] = grads_ref[a * SUB:(a + 1) * SUB, c * TC:(c + 1) * TC]


def pack(acts, grads):
    return pl.pallas_call(
        pack_kernel,
        grid=(DGRID // 4,),
        in_specs=[
            pl.BlockSpec((BLOCK, 4 * TR), lambda a: (0, a)),
            pl.BlockSpec((4 * SUB, HW), lambda a: (a, 0)),
        ],
        out_specs=pl.BlockSpec((4 * HGRID, SUB, TR + TC), lambda a: (a, 0, 0)),
        out_shape=jax.ShapeDtypeStruct((DGRID * HGRID, SUB, TR + TC), jnp.bfloat16),
    )(acts, grads)


def compact_kernel(cap, aidx, gidx, count, recv, acts_out, grads_out, asem, gsem):
    def acopy(k):
        return pltpu.make_async_copy(recv.at[aidx[k], :, pl.ds(0, TR)], acts_out.at[k], asem.at[k])

    def gcopy(k):
        return pltpu.make_async_copy(recv.at[gidx[k], :, pl.ds(TR, TC)], grads_out.at[k], gsem.at[k])

    def start(k, carry):
        gcopy(k).start()
        acopy(k).start()
        return carry

    def finish(k, carry):
        gcopy(k).wait()
        acopy(k).wait()
        return carry

    lax.fori_loop(0, cap, start, 0)
    lax.fori_loop(0, cap, finish, 0)

    def clear(k, carry):
        acts_out[k] = jnp.zeros((SUB, TR), jnp.bfloat16)
        return carry

    lax.fori_loop(count[0], cap, clear, 0)


def compact(cap, recv, aidx, gidx, count):
    smem = pl.BlockSpec(memory_space=pltpu.SMEM)
    vmem = pl.BlockSpec(memory_space=pltpu.VMEM)
    return pl.pallas_call(
        lambda *refs: compact_kernel(cap, *refs),
        in_specs=[smem, smem, smem, pl.BlockSpec(memory_space=pl.ANY)],
        out_specs=[vmem, vmem],
        out_shape=[
            jax.ShapeDtypeStruct((cap, SUB, TR), jnp.bfloat16),
            jax.ShapeDtypeStruct((cap, SUB, TC), jnp.bfloat16),
        ],
        scratch_shapes=[pltpu.SemaphoreType.DMA((cap,)), pltpu.SemaphoreType.DMA((cap,))],
    )(aidx, gidx, count, recv)


def order_of(touched):
    blocks = jnp.arange(BLOCKS)
    rank = jnp.sum((blocks[None, :] < blocks[:, None]) & touched[None, :], axis=1)
    hit = touched[None, :] & (rank[None, :] == blocks[:, None])
    return jnp.sum(jnp.where(hit, blocks[None, :], 0), axis=1).astype(jnp.int32)


def ring(axis, size, distance):
    return [(i, (i + distance) % size) for i in range(size)]


def product_kernel(n, scale, has_total, *refs):
    where, acts = refs[0], refs[1]
    pieces, rest = refs[2:2 + n], refs[2 + n:]
    out = rest[-1]

    def tile(t, carry):
        rows = pl.ds(pl.multiple_of(t * MTILE, MTILE), MTILE)
        total = rest[0][rows, :] if has_total else None
        for i in range(n):
            now = lax.dot_general(
                acts[where[i], :, rows], pieces[i][...],
                (((0,), (0,)), ((), ())), preferred_element_type=jnp.float32,
            )
            total = now if total is None else total + now
        out[rows, :] = (total * scale).astype(out.dtype)
        return carry

    lax.fori_loop(0, TR // MTILE, tile, 0)


def products(where, acts, pieces, total, dtype, scale=1.0):
    rows = acts.shape[1]
    vmem = pl.BlockSpec(memory_space=pltpu.VMEM)
    arrays = [acts] + [p.reshape(rows, TC) for p in pieces] + ([] if total is None else [total])
    return pl.pallas_call(
        lambda *refs: product_kernel(len(pieces), scale, total is not None, *refs),
        in_specs=[pl.BlockSpec(memory_space=pltpu.SMEM)] + [vmem] * len(arrays),
        out_specs=vmem,
        out_shape=jax.ShapeDtypeStruct((TR, TC), dtype),
        cost_estimate=pl.CostEstimate(
            flops=2 * len(pieces) * rows * TR * TC,
            bytes_accessed=len(pieces) * rows * (TR + TC) * 2 + 4 * TR * TC, transcendentals=0,
        ),
        compiler_params=pltpu.CompilerParams(vmem_limit_bytes=40 << 20),
    )(where, *arrays)


def gather_and_multiply(cap, recv, aidx, gidx, count, total, dtype, scale):
    y, zh, core = lax.axis_index("y"), lax.axis_index("zh"), lax.axis_index("core")
    acts_c, grads_c = compact(cap, recv, aidx, gidx, count)
    plane = [(z, c) for z in range(NZ) for c in range(2)]
    hop = [((z * 2 + c), (z + (2 if c == 0 else -2)) % NZ * 2 + c) for z, c in plane]
    far = lax.ppermute(grads_c, ("zh", "zl", "core"), hop)
    near = lax.ppermute(grads_c, "x", ring("x", NX, -1))
    far, near, acts_c = lax.optimization_barrier((far, near, acts_c))
    far = lax.ppermute(
        far, ("x", "zh", "zl", "core"),
        [(s * 2 * NZ + i, (s - 1) % NX * 2 * NZ + j) for s in range(NX) for i, j in hop],
    )
    acts_all = lax.all_gather(acts_c, ("zl", "core")).reshape(DGRID, cap * SUB, TR)

    def ring_step(sign):
        return [
            ((yy * NZ + z) * 2 + c, ((yy + (sign if c == 0 else -sign)) % NY * NZ + z) * 2 + c)
            for yy in range(NY) for z in range(NZ) for c in range(2)
        ]

    def around(own):
        first = lax.ppermute(own, DP, ring_step(1))
        second = lax.ppermute(own, DP, ring_step(-1))
        third = lax.ppermute(first, DP, ring_step(1))
        return first, second, third

    def places(flip):
        h = 1 - zh if flip else zh
        way = 1 - 2 * core
        return jnp.stack(
            [lax.rem(y + NY - d, NY) * 2 + h for d in (0, way, -way, 2)]
        ).astype(jnp.int32)

    first, second, third = around(near)
    far, second = lax.optimization_barrier((far, second))
    far_first, far_second, far_third = around(far)
    here, there = places(False), places(True)
    most = jnp.concatenate([here, there[:3]])
    pieces = (near, first, second, third, far, far_first, far_second)
    total = products(most, acts_all, pieces, total, jnp.float32)
    return products(there[3:], acts_all, (far_third,), total, dtype, scale)


def shards(acts, grad_rows, block_experts):
    packed = pack(acts[0], grad_rows[0])
    behind = [block_experts] + [
        lax.ppermute(block_experts, "x", ring("x", NX, d)) for d in (1, 2, 3)
    ]
    touched = [jnp.any(b[0] == 0, axis=1) for b in behind]
    counts = [jnp.sum(t.astype(jnp.int32)) for t in touched]
    most = jnp.maximum(jnp.maximum(counts[0], counts[1]), jnp.maximum(counts[2], counts[3]))
    aidx, gidx = (jnp.pad(order_of(t), (0, MORE)) for t in touched[:2])
    recv = lax.all_to_all(packed, DP, split_axis=0, concat_axis=0, tiled=True)

    scale = 2.0 / math.sqrt(BLOCKS * BLOCK)

    def straight(cap):
        def run(recv, aidx, gidx, count, most):
            return gather_and_multiply(
                cap, recv, aidx[:cap], gidx[:cap], jnp.minimum(count, cap), None, jnp.bfloat16, scale
            )
        return run

    def rounds(recv, aidx, gidx, count, most):
        def one(j, total):
            start = j * MORE
            return gather_and_multiply(
                MORE, recv,
                lax.dynamic_slice_in_dim(aidx, start, MORE),
                lax.dynamic_slice_in_dim(gidx, start, MORE),
                jnp.clip(count - start, 0, MORE), total, jnp.float32, 1.0,
            )

        turns = (most + MORE - 1) // MORE
        total = lax.fori_loop(0, turns, one, jnp.zeros((TR, TC), jnp.float32))
        return (total * scale).astype(jnp.bfloat16)

    out = lax.switch(
        (most > MAIN).astype(jnp.int32), [straight(MAIN), rounds],
        recv, aidx, gidx, counts[0].reshape(1), most,
    )
    return out[None, None]


def solution(mesh):
    fine = Mesh(mesh.devices.reshape(NX, NY, 2, 4, 2), ("x",) + DP)
    return jax.shard_map(
        shards,
        mesh=fine,
        in_specs=(P("x", DP, None), P("x", DP, None), P("x", None, None)),
        out_specs=P("x", DP, None, None),
        check_vma=False,
    )
```
